256 devices in a mesh: ctx: 32 (over x, z_hi, core), chan: 8 (over y, z_lo).
Axes of the slice: x: 4, y: 4, z: 8 (z_hi: 4, z_lo: 2; z = z_hi * 2 + z_lo), core: 2. Of those that a mesh axis runs over, the one named last changes fastest.
Arguments:
- grad_out: bfloat16 [256, 32768], P('chan', 'ctx'), may hold values from -6 to 6
- query: bfloat16 [256, 32768], P('chan', 'ctx'), may hold values from -6 to 6
- key_proj: bfloat16 [256, 32768], P('chan', 'ctx'), may hold values from -6 to 6
- value: bfloat16 [256, 32768], P('chan', 'ctx'), may hold values from -6 to 6
- filter_param: float32 [32, 32768], P(None, 'ctx'), may hold values from -6 to 6
Outputs:
- grad_query: bfloat16 [256, 32768], P('chan', 'ctx')
- grad_key: bfloat16 [256, 32768], P('chan', 'ctx')
- grad_value: bfloat16 [256, 32768], P('chan', 'ctx')
- grad_filter: float32 [32, 32768], P(None, 'ctx')
The draws below stay inside these ranges and needn't reach their ends.
All inputs are finite; a program needn't handle non-finite values.
Results may differ from the reference program's by a relative error of at most 0.004.
Values sent between devices are 32-bit elements; how exact they have to be, the bound alone decides.
No kernel may reach another device: no remote copies, remote signals or barrier semaphores. Data moves between devices by JAX's collectives and lax.ppermute only.
A program may use at most 128 MiB of HBM per device.

```python
import math
import jax
import jax.numpy as jnp

TOKENS = 32768
CHANNELS = 256
FILTERS = 32
N_CHAN = 8


def block_levels(own_key, extent, shards, least, high):
    gain, own = 1.0, jax.random.fold_in(own_key, 6)
    for dim, blocks in shards:
        steps = jnp.exp(jax.random.uniform(jax.random.fold_in(own, dim), (blocks,), jnp.float32, least / len(shards), high / len(shards)))
        gain = gain * jnp.repeat(steps, extent[dim] // blocks).reshape([-1 if axis == dim else 1 for axis in range(len(extent))])
    return gain


def normal_values(rng, shape, scale, reach, pieces=(), dtype=jnp.bfloat16):
    drawn = jax.random.normal(rng, shape, jnp.float32) * scale
    if len(pieces) > 0:
        drawn = block_levels(rng, shape, pieces, -0.22, 0.18) * drawn
    return jnp.clip(drawn, min=-reach, max=reach).astype(dtype)


def setup_inputs(seed: int = 0) -> dict:
    streams_of = jax.random.split(jax.random.key(seed), 6)
    grad_out = normal_values(streams_of[0], (CHANNELS, TOKENS), 1.0, 6.0, ((0, 8), (1, 32)))
    query = normal_values(streams_of[1], (CHANNELS, TOKENS), 1.0, 6.0, ((0, 8), (1, 32)))
    key_proj = normal_values(streams_of[2], (CHANNELS, TOKENS), 1.0, 6.0, ((0, 8), (1, 32)))
    value = normal_values(streams_of[3], (CHANNELS, TOKENS), 1.0, 6.0, ((0, 8), (1, 32)))
    filter_param = normal_values(streams_of[4], (FILTERS, TOKENS), 1.0, 6.0, ((1, 32),), jnp.float32)
    return {"grad_out": grad_out, "query": query, "key_proj": key_proj, "value": value, "filter_param": filter_param}


def reference(grad_out, query, key_proj, value, filter_param):
    filter_scale = 1.0 / math.sqrt(TOKENS)
    filt = filter_param.T * filter_scale
    padded = 2 * TOKENS
    filter_spec = jnp.fft.rfft(filt, n=padded, axis=0)
    dq_list = []
    dk_list = []
    dv_list = []
    filter_total = jnp.zeros((TOKENS, FILTERS), jnp.float32)
    for group in range(N_CHAN):
        first = group * FILTERS
        cot_in = grad_out[first:first + FILTERS, :].T.astype(jnp.float32)
        gate_q = query[first:first + FILTERS, :].T.astype(jnp.float32)
        gate_k = key_proj[first:first + FILTERS, :].T.astype(jnp.float32)
        gate_v = value[first:first + FILTERS, :].T.astype(jnp.float32)
        signal = gate_k * gate_v
        cot = cot_in * gate_q
        signal_spec = jnp.fft.rfft(signal, n=padded, axis=0)
        cot_spec = jnp.fft.rfft(cot, n=padded, axis=0)
        conv = jnp.fft.irfft(filter_spec * signal_spec, n=padded, axis=0)[:TOKENS]
        grad_signal = jnp.fft.irfft(jnp.conj(filter_spec) * cot_spec, n=padded, axis=0)[:TOKENS]
        filter_total = filter_total + jnp.fft.irfft(cot_spec * jnp.conj(signal_spec), n=padded, axis=0)[:TOKENS]
        dq_list.append((cot_in * conv).T.astype(jnp.bfloat16))
        dk_list.append((grad_signal * gate_v).T.astype(jnp.bfloat16))
        dv_list.append((grad_signal * gate_k).T.astype(jnp.bfloat16))
    grad_query = jnp.concatenate(dq_list, axis=0)
    grad_key = jnp.concatenate(dk_list, axis=0)
    grad_value = jnp.concatenate(dv_list, axis=0)
    grad_filter = (filter_total * filter_scale).T
    return (grad_query, grad_key, grad_value, grad_filter)
```

```python
import math

import jax
import jax.numpy as jnp
import ml_dtypes
import numpy as np
from jax import lax
from jax.experimental import pallas as pl
from jax.experimental.pallas import tpu as pltpu
from jax.sharding import PartitionSpec as P

LANES = 128
SUBLANES = 8


def split_table(table):
    high = table.astype(np.float32).astype(ml_dtypes.bfloat16)
    low = (table - high.astype(np.float64)).astype(ml_dtypes.bfloat16)
    return high, low


def transform_tables(tokens):
    length = 2 * tokens
    rows = length // LANES
    half = rows // 2
    k1 = np.arange(half, dtype=np.float64) + 0.5
    n1 = np.arange(half, dtype=np.float64)
    n2 = np.arange(LANES, dtype=np.float64)
    outer = 2.0 * np.pi * k1[:, None] * n1[None, :] / rows
    first = np.concatenate([np.cos(outer), -np.sin(outer)], axis=0)
    last = first.T * (2.0 / length)
    twist = 2.0 * np.pi * k1[:, None] * n2[None, :] / length
    twist_cos = np.cos(twist).astype(np.float32)
    twist_sin = (-np.sin(twist)).astype(np.float32)
    inner = 2.0 * np.pi * n2[:, None] * n2[None, :] / LANES
    cos, sin = np.cos(inner), np.sin(inner)
    ahead = np.block([[cos, -sin], [sin, cos]])
    back = np.block([[cos, sin], [-sin, cos]])
    return split_table(first) + split_table(ahead) + split_table(back) + split_table(last) + (twist_cos, twist_sin)


def gate_kernel(grad_out, query, key_proj, value, filter_param, out, *, filter_scale):
    f32 = jnp.float32
    channels, here = key_proj.shape
    pieces = here // LANES
    stride = 3 * pieces
    parts = (
        key_proj[...].astype(f32) * value[...].astype(f32),
        grad_out[...].astype(f32) * query[...].astype(f32),
        filter_param[...] * filter_scale,
    )
    for index, part in enumerate(parts):
        for piece in range(pieces):
            out[pl.ds(index * pieces + piece, channels, stride=stride), :] = part[:, piece * LANES : (piece + 1) * LANES]


def split(values):
    high = values.astype(jnp.bfloat16)
    low = (values - high.astype(jnp.float32)).astype(jnp.bfloat16)
    return high, low


def product(left, right):
    def dot(a, b):
        return jnp.dot(a, b, preferred_element_type=jnp.float32)

    return dot(left[0], right[0]) + (dot(left[0], right[1]) + dot(left[1], right[0]))


def spectral_kernel(
    taken, first_h, first_l, ahead_h, ahead_l, back_h, back_l, last_h, last_l, twist_cos, twist_sin, out, *, filter_scale
):
    shards = taken.shape[0]
    pieces = taken.shape[1] // 3
    half = shards * pieces
    cos, sin = twist_cos[...], twist_sin[...]
    stacked = jnp.concatenate(
        [taken[:, i * pieces : (i + 1) * pieces, :].reshape(half, LANES) for i in range(3)], axis=1
    )
    mixed = product((first_h[...], first_l[...]), split(stacked))
    specs = []
    for i in range(3):
        real, imag = mixed[:half, i * LANES : (i + 1) * LANES], mixed[half:, i * LANES : (i + 1) * LANES]
        turned = jnp.concatenate([real * cos - imag * sin, real * sin + imag * cos], axis=1)
        spec = product(split(turned), (ahead_h[...], ahead_l[...]))
        specs.append((spec[:, :LANES], spec[:, LANES:]))
    (sig_re, sig_im), (cot_re, cot_im), (filt_re, filt_im) = specs
    results = (
        (filt_re * sig_re - filt_im * sig_im, filt_re * sig_im + filt_im * sig_re),
        (filt_re * cot_re + filt_im * cot_im, filt_re * cot_im - filt_im * cot_re),
        (
            (cot_re * sig_re + cot_im * sig_im) * filter_scale,
            (cot_im * sig_re - cot_re * sig_im) * filter_scale,
        ),
    )
    columns = []
    for result in results:
        spec = product(split(jnp.concatenate(result, axis=1)), (back_h[...], back_l[...]))
        real, imag = spec[:, :LANES], spec[:, LANES:]
        columns.append(jnp.concatenate([real * cos + imag * sin, imag * cos - real * sin], axis=0))
    timed = product((last_h[...], last_l[...]), split(jnp.concatenate(columns, axis=1)))
    for i in range(3):
        out[:, i * pieces : (i + 1) * pieces, :] = timed[:, i * LANES : (i + 1) * LANES].reshape(shards, pieces, LANES)


def grads_kernel(back, grad_out, key_proj, value, grad_query, grad_key, grad_value):
    f32 = jnp.float32
    channels, here = key_proj.shape
    pieces = here // LANES
    stride = 3 * pieces
    for piece in range(pieces):
        columns = slice(piece * LANES, (piece + 1) * LANES)
        conv = back[pl.ds(piece, channels, stride=stride), :]
        grad_signal = back[pl.ds(pieces + piece, channels, stride=stride), :]
        grad_query[:, columns] = (grad_out[:, columns].astype(f32) * conv).astype(jnp.bfloat16)
        grad_key[:, columns] = (grad_signal * value[:, columns].astype(f32)).astype(jnp.bfloat16)
        grad_value[:, columns] = (grad_signal * key_proj[:, columns].astype(f32)).astype(jnp.bfloat16)


def total_kernel(first, second, third, fourth, out):
    channels, here = out.shape
    pieces = here // LANES
    for piece in range(pieces):
        rows = pl.ds(piece, channels, stride=pieces)
        out[:, piece * LANES : (piece + 1) * LANES] = (first[rows, :] + second[rows, :]) + (third[rows, :] + fourth[rows, :])


def local(grad_out, query, key_proj, value, filter_param):
    f32 = jnp.float32
    shards = lax.axis_size("ctx")
    groups = lax.axis_size("chan")
    channels, here = grad_out.shape
    tokens = shards * here
    pieces = here // LANES
    filter_scale = 1.0 / math.sqrt(tokens)
    params = pltpu.CompilerParams(vmem_limit_bytes=24 * 1024 * 1024)
    gated = pl.pallas_call(
        lambda *refs: gate_kernel(*refs, filter_scale=filter_scale),
        out_shape=jax.ShapeDtypeStruct((channels * 3 * pieces, LANES), f32),
        compiler_params=params,
        name="gate",
    )(grad_out, query, key_proj, value, filter_param)
    taken = lax.all_to_all(gated.reshape(channels, 3 * pieces, LANES), "ctx", 0, 0, tiled=True)
    tables = [jnp.asarray(table) for table in transform_tables(tokens)]
    timed = pl.pallas_call(
        lambda *refs: spectral_kernel(*refs, filter_scale=filter_scale),
        out_shape=jax.ShapeDtypeStruct((shards, 3 * pieces, LANES), f32),
        compiler_params=params,
        name="spectral",
    )(taken, *tables)
    back = lax.all_to_all(timed, "ctx", 0, 0, tiled=True)
    partial = back[:, 2 * pieces :, :].reshape(channels * pieces, LANES)
    pair = partial + lax.ppermute(partial, "chan", [(i, i ^ 1) for i in range(groups)])
    others = [
        lax.ppermute(pair, "chan", [(i, (i + 2 * step) % groups) for i in range(groups)]) for step in range(1, groups // 2)
    ]
    grad_query, grad_key, grad_value = pl.pallas_call(
        grads_kernel,
        out_shape=[jax.ShapeDtypeStruct((channels, here), jnp.bfloat16)] * 3,
        compiler_params=params,
        name="grads",
    )(back.reshape(channels * 3 * pieces, LANES), grad_out, key_proj, value)
    grad_filter = pl.pallas_call(
        total_kernel,
        out_shape=jax.ShapeDtypeStruct((channels, here), f32),
        compiler_params=params,
        name="total",
    )(pair, *others)
    return (grad_query, grad_key, grad_value, grad_filter)


def solution(mesh):
    split_spec = P("chan", "ctx")
    in_specs = (split_spec, split_spec, split_spec, split_spec, P(None, "ctx"))
    out_specs = (split_spec, split_spec, split_spec, P(None, "ctx"))
    return jax.shard_map(local, mesh=mesh, in_specs=in_specs, out_specs=out_specs, check_vma=False)
```

```python
import math

import jax
import jax.numpy as jnp
import ml_dtypes
import numpy as np
from jax import lax
from jax.experimental import pallas as pl
from jax.experimental.pallas import tpu as pltpu
from jax.sharding import PartitionSpec as P

LANES = 128
SUBLANES = 8


def split_table(table):
    high = table.astype(np.float32).astype(ml_dtypes.bfloat16)
    low = (table - high.astype(np.float64)).astype(ml_dtypes.bfloat16)
    return high, low


def transform_tables(tokens):
    length = 2 * tokens
    rows = length // LANES
    half = rows // 2
    k1 = np.arange(half, dtype=np.float64) + 0.5
    n1 = np.arange(half, dtype=np.float64)
    n2 = np.arange(LANES, dtype=np.float64)
    outer = 2.0 * np.pi * k1[:, None] * n1[None, :] / rows
    cos, sin = np.cos(outer), np.sin(outer)
    first = np.concatenate([cos, -sin], axis=0)
    last = np.concatenate([cos.T, sin.T], axis=1) * (2.0 / length)
    twist = 2.0 * np.pi * k1[:, None] * n2[None, :] / length
    twists = np.concatenate([np.cos(twist), -np.sin(twist)], axis=1).astype(np.float32)
    inner = 2.0 * np.pi * n2[:, None] * n2[None, :] / LANES
    cos, sin = np.cos(inner), np.sin(inner)
    second = np.block([[cos, -sin], [sin, cos]])
    return split_table(first) + split_table(second) + split_table(last) + (twists,)


def gate_kernel(grad_out, query, key_proj, value, filter_param, out, go, q, k, v, filt, sems, *, filter_scale):
    f32 = jnp.float32
    channels, here = key_proj.shape
    pieces = here // LANES
    stride = 3 * pieces
    pairs = ((key_proj, k), (value, v), (grad_out, go), (query, q), (filter_param, filt))
    copies = [pltpu.make_async_copy(source, held, sems.at[i]) for i, (source, held) in enumerate(pairs)]
    for copy in copies:
        copy.start()

    def place(index, part):
        for piece in range(pieces):
            out[pl.ds(index * pieces + piece, channels, stride=stride), :] = part[:, piece * LANES : (piece + 1) * LANES]

    copies[0].wait()
    copies[1].wait()
    place(0, k[...].astype(f32) * v[...].astype(f32))
    copies[2].wait()
    copies[3].wait()
    place(1, go[...].astype(f32) * q[...].astype(f32))
    copies[4].wait()
    place(2, filt[...] * filter_scale)


def split(values):
    high = values.astype(jnp.bfloat16)
    low = (values - high.astype(jnp.float32)).astype(jnp.bfloat16)
    return high, low


def product(left, right):
    def dot(a, b):
        return jnp.dot(a, b, preferred_element_type=jnp.float32)

    return dot(left[0], right[0]) + (dot(left[0], right[1]) + dot(left[1], right[0]))


def spectral_kernel(taken, first_h, first_l, second_h, second_l, last_h, last_l, twists, out, *, filter_scale):
    shards = taken.shape[0]
    pieces = taken.shape[1] // 3
    half = shards * pieces
    cos, sin = twists[:, :LANES], twists[:, LANES:]
    stacked = jnp.concatenate(
        [taken[:, i * pieces : (i + 1) * pieces, :].reshape(half, LANES) for i in range(3)], axis=1
    )
    mixed = product((first_h[...], first_l[...]), split(stacked))
    specs = []
    for i in range(3):
        real, imag = mixed[:half, i * LANES : (i + 1) * LANES], mixed[half:, i * LANES : (i + 1) * LANES]
        turned = jnp.concatenate([real * cos - imag * sin, real * sin + imag * cos], axis=1)
        spec = product(split(turned), (second_h[...], second_l[...]))
        specs.append((spec[:, :LANES], spec[:, LANES:]))
    (sig_re, sig_im), (cot_re, cot_im), (filt_re, filt_im) = specs
    results = (
        (filt_re * sig_re - filt_im * sig_im, -(filt_re * sig_im + filt_im * sig_re)),
        (filt_re * cot_re + filt_im * cot_im, filt_im * cot_re - filt_re * cot_im),
        (
            (cot_re * sig_re + cot_im * sig_im) * filter_scale,
            (cot_re * sig_im - cot_im * sig_re) * filter_scale,
        ),
    )
    columns = []
    for result in results:
        spec = product(split(jnp.concatenate(result, axis=1)), (second_h[...], second_l[...]))
        real, imag = spec[:, :LANES], spec[:, LANES:]
        columns.append(jnp.concatenate([real * cos - imag * sin, real * sin + imag * cos], axis=0))
    timed = product((last_h[...], last_l[...]), split(jnp.concatenate(columns, axis=1)))
    for i in range(3):
        out[:, i * pieces : (i + 1) * pieces, :] = timed[:, i * LANES : (i + 1) * LANES].reshape(shards, pieces, LANES)


def grads_kernel(back, grad_out, key_proj, value, grad_query, grad_key, grad_value):
    f32 = jnp.float32
    channels, here = key_proj.shape
    pieces = here // LANES
    stride = 3 * pieces
    for piece in range(pieces):
        columns = slice(piece * LANES, (piece + 1) * LANES)
        conv = back[pl.ds(piece, channels, stride=stride), :]
        grad_signal = back[pl.ds(pieces + piece, channels, stride=stride), :]
        grad_query[:, columns] = (grad_out[:, columns].astype(f32) * conv).astype(jnp.bfloat16)
        grad_key[:, columns] = (grad_signal * value[:, columns].astype(f32)).astype(jnp.bfloat16)
        grad_value[:, columns] = (grad_signal * key_proj[:, columns].astype(f32)).astype(jnp.bfloat16)


def total_kernel(first, second, third, fourth, out):
    channels, here = out.shape
    pieces = here // LANES
    for piece in range(pieces):
        rows = pl.ds(piece, channels, stride=pieces)
        out[:, piece * LANES : (piece + 1) * LANES] = (first[rows, :] + second[rows, :]) + (third[rows, :] + fourth[rows, :])


def local(grad_out, query, key_proj, value, filter_param):
    f32 = jnp.float32
    shards = lax.axis_size("ctx")
    groups = lax.axis_size("chan")
    channels, here = grad_out.shape
    tokens = shards * here
    pieces = here // LANES
    filter_scale = 1.0 / math.sqrt(tokens)
    params = pltpu.CompilerParams(vmem_limit_bytes=24 * 1024 * 1024)
    gated = pl.pallas_call(
        lambda *refs: gate_kernel(*refs, filter_scale=filter_scale),
        out_shape=jax.ShapeDtypeStruct((channels * 3 * pieces, LANES), f32),
        in_specs=[pl.BlockSpec(memory_space=pltpu.HBM)] * 5,
        scratch_shapes=[pltpu.VMEM((channels, here), jnp.bfloat16)] * 4
        + [pltpu.VMEM((channels, here), f32), pltpu.SemaphoreType.DMA((5,))],
        name="gate",
    )(grad_out, query, key_proj, value, filter_param)
    taken = lax.all_to_all(gated.reshape(channels, 3 * pieces, LANES), "ctx", 0, 0, tiled=True)
    tables = [jnp.asarray(table) for table in transform_tables(tokens)]
    timed = pl.pallas_call(
        lambda *refs: spectral_kernel(*refs, filter_scale=filter_scale),
        out_shape=jax.ShapeDtypeStruct((shards, 3 * pieces, LANES), f32),
        compiler_params=params,
        name="spectral",
    )(taken, *tables)
    back = lax.all_to_all(timed, "ctx", 0, 0, tiled=True)
    partial = back[:, 2 * pieces :, :].reshape(channels * pieces, LANES)
    pair = partial + lax.ppermute(partial, "chan", [(i, i ^ 1) for i in range(groups)])
    others = [
        lax.ppermute(pair, "chan", [(i, (i + 2 * step) % groups) for i in range(groups)]) for step in range(1, groups // 2)
    ]
    grad_query, grad_key, grad_value = pl.pallas_call(
        grads_kernel,
        out_shape=[jax.ShapeDtypeStruct((channels, here), jnp.bfloat16)] * 3,
        compiler_params=params,
        name="grads",
    )(back.reshape(channels * 3 * pieces, LANES), grad_out, key_proj, value)
    grad_filter = pl.pallas_call(
        total_kernel,
        out_shape=jax.ShapeDtypeStruct((channels, here), f32),
        compiler_params=params,
        name="total",
    )(pair, *others)
    return (grad_query, grad_key, grad_value, grad_filter)


def solution(mesh):
    split_spec = P("chan", "ctx")
    in_specs = (split_spec, split_spec, split_spec, split_spec, P(None, "ctx"))
    out_specs = (split_spec, split_spec, split_spec, P(None, "ctx"))
    return jax.shard_map(local, mesh=mesh, in_specs=in_specs, out_specs=out_specs, check_vma=False)
```

```python
import math

import jax
import jax.numpy as jnp
import ml_dtypes
import numpy as np
from jax import lax
from jax.experimental import pallas as pl
from jax.experimental.pallas import tpu as pltpu
from jax.sharding import PartitionSpec as P

LANES = 128
SUBLANES = 8


def split_table(table):
    high = table.astype(np.float32).astype(ml_dtypes.bfloat16)
    low = (table - high.astype(np.float64)).astype(ml_dtypes.bfloat16)
    return high, low


def transform_tables(tokens):
    length = 2 * tokens
    rows = length // LANES
    half = rows // 2
    k1 = np.arange(half, dtype=np.float64) + 0.5
    n1 = np.arange(half, dtype=np.float64)
    n2 = np.arange(LANES, dtype=np.float64)
    outer = 2.0 * np.pi * k1[:, None] * n1[None, :] / rows
    cos, sin = np.cos(outer), np.sin(outer)
    first = np.concatenate([cos, -sin], axis=0)
    last = np.concatenate([cos.T, sin.T], axis=1) * (2.0 / length)
    twist = 2.0 * np.pi * k1[:, None] * n2[None, :] / length
    twists = np.concatenate([np.cos(twist), -np.sin(twist)], axis=1).astype(np.float32)
    inner = 2.0 * np.pi * n2[:, None] * n2[None, :] / LANES
    cos, sin = np.cos(inner), np.sin(inner)
    second = np.block([[cos, -sin], [sin, cos]])
    return split_table(first) + split_table(second) + split_table(last) + (twists,)


def gate_kernel(grad_out, query, key_proj, value, filter_param, out, go, q, k, v, filt, sems, *, filter_scale):
    f32 = jnp.float32
    channels, here = key_proj.shape
    pieces = here // LANES
    stride = 3 * pieces
    pairs = ((key_proj, k), (value, v), (grad_out, go), (query, q), (filter_param, filt))
    copies = [pltpu.make_async_copy(source, held, sems.at[i]) for i, (source, held) in enumerate(pairs)]
    for copy in copies:
        copy.start()

    def place(index, part):
        for piece in range(pieces):
            out[pl.ds(index * pieces + piece, channels, stride=stride), :] = part[:, piece * LANES : (piece + 1) * LANES]

    copies[0].wait()
    copies[1].wait()
    place(0, k[...].astype(f32) * v[...].astype(f32))
    copies[2].wait()
    copies[3].wait()
    place(1, go[...].astype(f32) * q[...].astype(f32))
    copies[4].wait()
    place(2, filt[...] * filter_scale)


def split(values):
    high = values.astype(jnp.bfloat16)
    low = (values - high.astype(jnp.float32)).astype(jnp.bfloat16)
    return high, low


def product(left, right):
    def dot(a, b):
        return jnp.dot(a, b, preferred_element_type=jnp.float32)

    return dot(left[0], right[0]) + (dot(left[0], right[1]) + dot(left[1], right[0]))


def spectral_kernel(taken, first_h, first_l, second_h, second_l, last_h, last_l, twists, out, *, filter_scale):
    shards = taken.shape[0]
    pieces = taken.shape[1] // 3
    half = shards * pieces
    cos, sin = twists[:, :LANES], twists[:, LANES:]
    stacked = jnp.concatenate(
        [taken[:, i * pieces : (i + 1) * pieces, :].reshape(half, LANES) for i in range(3)], axis=1
    )
    mixed = product((first_h[...], first_l[...]), split(stacked))
    specs = []
    for i in range(3):
        real, imag = mixed[:half, i * LANES : (i + 1) * LANES], mixed[half:, i * LANES : (i + 1) * LANES]
        turned = jnp.concatenate([real * cos - imag * sin, real * sin + imag * cos], axis=1)
        spec = product(split(turned), (second_h[...], second_l[...]))
        specs.append((spec[:, :LANES], spec[:, LANES:]))
    (sig_re, sig_im), (cot_re, cot_im), (filt_re, filt_im) = specs
    results = (
        (filt_re * sig_re - filt_im * sig_im, -(filt_re * sig_im + filt_im * sig_re)),
        (filt_re * cot_re + filt_im * cot_im, filt_im * cot_re - filt_re * cot_im),
        (
            (cot_re * sig_re + cot_im * sig_im) * filter_scale,
            (cot_re * sig_im - cot_im * sig_re) * filter_scale,
        ),
    )
    columns = []
    for result in results:
        spec = product(split(jnp.concatenate(result, axis=1)), (second_h[...], second_l[...]))
        real, imag = spec[:, :LANES], spec[:, LANES:]
        columns.append(jnp.concatenate([real * cos - imag * sin, real * sin + imag * cos], axis=0))
    timed = product((last_h[...], last_l[...]), split(jnp.concatenate(columns, axis=1)))
    for i in range(3):
        out[:, i * pieces : (i + 1) * pieces, :] = timed[:, i * LANES : (i + 1) * LANES].reshape(shards, pieces, LANES)


def grads_kernel(back, grad_out, key_proj, value, grad_query, grad_key, grad_value):
    f32 = jnp.float32
    channels, here = key_proj.shape
    pieces = here // LANES
    stride = 3 * pieces
    for piece in range(pieces):
        columns = slice(piece * LANES, (piece + 1) * LANES)
        conv = back[pl.ds(piece, channels, stride=stride), :]
        grad_signal = back[pl.ds(pieces + piece, channels, stride=stride), :]
        grad_query[:, columns] = (grad_out[:, columns].astype(f32) * conv).astype(jnp.bfloat16)
        grad_key[:, columns] = (grad_signal * value[:, columns].astype(f32)).astype(jnp.bfloat16)
        grad_value[:, columns] = (grad_signal * key_proj[:, columns].astype(f32)).astype(jnp.bfloat16)


def total_kernel(first, second, third, fourth, out):
    channels, here = out.shape
    pieces = here // LANES
    for piece in range(pieces):
        rows = pl.ds(piece, channels, stride=pieces)
        out[:, piece * LANES : (piece + 1) * LANES] = (first[rows, :] + second[rows, :]) + (third[rows, :] + fourth[rows, :])


def local(grad_out, query, key_proj, value, filter_param):
    f32 = jnp.float32
    shards = lax.axis_size("ctx")
    groups = lax.axis_size("chan")
    channels, here = grad_out.shape
    tokens = shards * here
    pieces = here // LANES
    filter_scale = 1.0 / math.sqrt(tokens)
    params = pltpu.CompilerParams(vmem_limit_bytes=24 * 1024 * 1024)
    gated = pl.pallas_call(
        lambda *refs: gate_kernel(*refs, filter_scale=filter_scale),
        out_shape=jax.ShapeDtypeStruct((channels * 3 * pieces, LANES), f32),
        in_specs=[pl.BlockSpec(memory_space=pltpu.HBM)] * 5,
        scratch_shapes=[pltpu.VMEM((channels, here), jnp.bfloat16)] * 4
        + [pltpu.VMEM((channels, here), f32), pltpu.SemaphoreType.DMA((5,))],
        compiler_params=params,
        name="gate",
    )(*[pltpu.with_memory_space_constraint(each, pltpu.HBM) for each in (grad_out, query, key_proj, value, filter_param)])
    taken = lax.all_to_all(gated.reshape(channels, 3 * pieces, LANES), "ctx", 0, 0, tiled=True)
    tables = [jnp.asarray(table) for table in transform_tables(tokens)]
    timed = pl.pallas_call(
        lambda *refs: spectral_kernel(*refs, filter_scale=filter_scale),
        out_shape=jax.ShapeDtypeStruct((shards, 3 * pieces, LANES), f32),
        compiler_params=params,
        name="spectral",
    )(taken, *tables)
    back = lax.all_to_all(timed, "ctx", 0, 0, tiled=True)
    partial = back[:, 2 * pieces :, :].reshape(channels * pieces, LANES)
    pair = partial + lax.ppermute(partial, "chan", [(i, i ^ 1) for i in range(groups)])
    others = [
        lax.ppermute(pair, "chan", [(i, (i + 2 * step) % groups) for i in range(groups)]) for step in range(1, groups // 2)
    ]
    grad_query, grad_key, grad_value = pl.pallas_call(
        grads_kernel,
        out_shape=[jax.ShapeDtypeStruct((channels, here), jnp.bfloat16)] * 3,
        compiler_params=params,
        name="grads",
    )(back.reshape(channels * 3 * pieces, LANES), grad_out, key_proj, value)
    grad_filter = pl.pallas_call(
        total_kernel,
        out_shape=jax.ShapeDtypeStruct((channels, here), f32),
        compiler_params=params,
        name="total",
    )(pair, *others)
    return (grad_query, grad_key, grad_value, grad_filter)


def solution(mesh):
    split_spec = P("chan", "ctx")
    in_specs = (split_spec, split_spec, split_spec, split_spec, P(None, "ctx"))
    out_specs = (split_spec, split_spec, split_spec, P(None, "ctx"))
    return jax.shard_map(local, mesh=mesh, in_specs=in_specs, out_specs=out_specs, check_vma=False)
```

```python
import math

import jax
import jax.numpy as jnp
import ml_dtypes
import numpy as np
from jax import lax
from jax.experimental import pallas as pl
from jax.experimental.pallas import tpu as pltpu
from jax.sharding import PartitionSpec as P

LANES = 128
SUBLANES = 8


def split_table(table):
    high = table.astype(np.float32).astype(ml_dtypes.bfloat16)
    low = (table - high.astype(np.float64)).astype(ml_dtypes.bfloat16)
    return high, low


def transform_tables(tokens):
    length = 2 * tokens
    rows = length // LANES
    half = rows // 2
    k1 = np.arange(half, dtype=np.float64) + 0.5
    n1 = np.arange(half, dtype=np.float64)
    n2 = np.arange(LANES, dtype=np.float64)
    outer = 2.0 * np.pi * k1[:, None] * n1[None, :] / rows
    cos, sin = np.cos(outer), np.sin(outer)
    first = np.concatenate([cos, -sin], axis=0)
    last = np.concatenate([cos.T, sin.T], axis=1) * (2.0 / length)
    twist = 2.0 * np.pi * k1[:, None] * n2[None, :] / length
    twists = np.concatenate([np.cos(twist), -np.sin(twist)], axis=1).astype(np.float32)
    inner = 2.0 * np.pi * n2[:, None] * n2[None, :] / LANES
    cos, sin = np.cos(inner), np.sin(inner)
    second = np.block([[cos, -sin], [sin, cos]])
    return split_table(first) + split_table(second) + split_table(last) + (twists,)


def gate_kernel(grad_out, query, key_proj, value, filter_param, out, go, q, k, v, filt, sems, *, filter_scale):
    f32 = jnp.float32
    channels, here = key_proj.shape
    pieces = here // LANES
    stride = 3 * pieces
    pairs = ((key_proj, k), (value, v), (grad_out, go), (query, q), (filter_param, filt))
    copies = [pltpu.make_async_copy(source, held, sems.at[i]) for i, (source, held) in enumerate(pairs)]
    for copy in copies:
        copy.start()

    def place(index, part):
        for piece in range(pieces):
            out[pl.ds(index * pieces + piece, channels, stride=stride), :] = part[:, piece * LANES : (piece + 1) * LANES]

    copies[0].wait()
    copies[1].wait()
    place(0, k[...].astype(f32) * v[...].astype(f32))
    copies[2].wait()
    copies[3].wait()
    place(1, go[...].astype(f32) * q[...].astype(f32))
    copies[4].wait()
    place(2, filt[...] * filter_scale)


def split(values):
    high = values.astype(jnp.bfloat16)
    low = (values - high.astype(jnp.float32)).astype(jnp.bfloat16)
    return high, low


def dot(left, right):
    return jnp.dot(left, right, preferred_element_type=jnp.float32)


def times_table(values, table):
    high, low = split(values)
    table_high, table_low = table
    return dot(high, table_high) + (dot(high, table_low) + dot(low, table_high))


def table_times(table, columns):
    table_high, table_low = table
    parts = [split(column) for column in columns]
    lows = dot(table_low, jnp.concatenate([high for high, _ in parts], axis=1))
    results = []
    for i, part in enumerate(parts):
        both = dot(table_high, jnp.concatenate(part, axis=1))
        results.append(both[:, :LANES] + (both[:, LANES:] + lows[:, i * LANES : (i + 1) * LANES]))
    return results


def spectral_kernel(taken, first_h, first_l, second_h, second_l, last_h, last_l, twists, out, *, filter_scale):
    shards = taken.shape[0]
    pieces = taken.shape[1] // 3
    half = shards * pieces
    cos, sin = twists[:, :LANES], twists[:, LANES:]
    first, second, last = (first_h[...], first_l[...]), (second_h[...], second_l[...]), (last_h[...], last_l[...])

    def turn(real, imag):
        return real * cos - imag * sin, real * sin + imag * cos

    mixed = table_times(first, [taken[:, i * pieces : (i + 1) * pieces, :].reshape(half, LANES) for i in range(3)])
    specs = []
    for each in mixed:
        spec = times_table(jnp.concatenate(turn(each[:half], each[half:]), axis=1), second)
        specs.append((spec[:, :LANES], spec[:, LANES:]))
    (sig_re, sig_im), (cot_re, cot_im), (filt_re, filt_im) = specs
    results = (
        (filt_re * sig_re - filt_im * sig_im, -(filt_re * sig_im + filt_im * sig_re)),
        (filt_re * cot_re + filt_im * cot_im, filt_im * cot_re - filt_re * cot_im),
        (
            (cot_re * sig_re + cot_im * sig_im) * filter_scale,
            (cot_re * sig_im - cot_im * sig_re) * filter_scale,
        ),
    )
    order = (2, 0, 1)
    columns = []
    for i in order:
        spec = times_table(jnp.concatenate(results[i], axis=1), second)
        columns.append(jnp.concatenate(turn(spec[:, :LANES], spec[:, LANES:]), axis=0))
    for i, timed in zip(order, table_times(last, columns)):
        out[:, i * pieces : (i + 1) * pieces, :] = timed.reshape(shards, pieces, LANES)


def grads_kernel(back, grad_out, key_proj, value, grad_query, grad_key, grad_value):
    f32 = jnp.float32
    channels, here = key_proj.shape
    pieces = here // LANES
    stride = 3 * pieces
    for piece in range(pieces):
        columns = slice(piece * LANES, (piece + 1) * LANES)
        conv = back[pl.ds(piece, channels, stride=stride), :]
        grad_signal = back[pl.ds(pieces + piece, channels, stride=stride), :]
        grad_query[:, columns] = (grad_out[:, columns].astype(f32) * conv).astype(jnp.bfloat16)
        grad_key[:, columns] = (grad_signal * value[:, columns].astype(f32)).astype(jnp.bfloat16)
        grad_value[:, columns] = (grad_signal * key_proj[:, columns].astype(f32)).astype(jnp.bfloat16)


def total_kernel(first, second, third, fourth, out):
    channels, here = out.shape
    pieces = here // LANES
    for piece in range(pieces):
        rows = pl.ds(piece, channels, stride=pieces)
        out[:, piece * LANES : (piece + 1) * LANES] = (first[rows, :] + second[rows, :]) + (third[rows, :] + fourth[rows, :])


def local(grad_out, query, key_proj, value, filter_param):
    f32 = jnp.float32
    shards = lax.axis_size("ctx")
    groups = lax.axis_size("chan")
    channels, here = grad_out.shape
    tokens = shards * here
    pieces = here // LANES
    filter_scale = 1.0 / math.sqrt(tokens)
    params = pltpu.CompilerParams(vmem_limit_bytes=24 * 1024 * 1024)
    gated = pl.pallas_call(
        lambda *refs: gate_kernel(*refs, filter_scale=filter_scale),
        out_shape=jax.ShapeDtypeStruct((channels * 3 * pieces, LANES), f32),
        in_specs=[pl.BlockSpec(memory_space=pltpu.HBM)] * 5,
        scratch_shapes=[pltpu.VMEM((channels, here), jnp.bfloat16)] * 4
        + [pltpu.VMEM((channels, here), f32), pltpu.SemaphoreType.DMA((5,))],
        compiler_params=params,
        name="gate",
    )(*[pltpu.with_memory_space_constraint(each, pltpu.HBM) for each in (grad_out, query, key_proj, value, filter_param)])
    taken = lax.all_to_all(gated.reshape(channels, 3 * pieces, LANES), "ctx", 0, 0, tiled=True)
    tables = [jnp.asarray(table) for table in transform_tables(tokens)]
    timed = pl.pallas_call(
        lambda *refs: spectral_kernel(*refs, filter_scale=filter_scale),
        out_shape=jax.ShapeDtypeStruct((shards, 3 * pieces, LANES), f32),
        compiler_params=params,
        name="spectral",
    )(taken, *tables)
    back = lax.all_to_all(timed, "ctx", 0, 0, tiled=True)
    partial = back[:, 2 * pieces :, :].reshape(channels * pieces, LANES)
    pair = partial + lax.ppermute(partial, "chan", [(i, i ^ 1) for i in range(groups)])
    others = [
        lax.ppermute(pair, "chan", [(i, (i + 2 * step) % groups) for i in range(groups)]) for step in range(1, groups // 2)
    ]
    grad_query, grad_key, grad_value = pl.pallas_call(
        grads_kernel,
        out_shape=[jax.ShapeDtypeStruct((channels, here), jnp.bfloat16)] * 3,
        compiler_params=params,
        name="grads",
    )(back.reshape(channels * 3 * pieces, LANES), grad_out, key_proj, value)
    grad_filter = pl.pallas_call(
        total_kernel,
        out_shape=jax.ShapeDtypeStruct((channels, here), f32),
        compiler_params=params,
        name="total",
    )(pair, *others)
    return (grad_query, grad_key, grad_value, grad_filter)


def solution(mesh):
    split_spec = P("chan", "ctx")
    in_specs = (split_spec, split_spec, split_spec, split_spec, P(None, "ctx"))
    out_specs = (split_spec, split_spec, split_spec, P(None, "ctx"))
    return jax.shard_map(local, mesh=mesh, in_specs=in_specs, out_specs=out_specs, check_vma=False)
```

```python
import math

import jax
import jax.numpy as jnp
import ml_dtypes
import numpy as np
from jax import lax
from jax.experimental import pallas as pl
from jax.experimental.pallas import tpu as pltpu
from jax.sharding import PartitionSpec as P

LANES = 128
SUBLANES = 8


def split_table(table):
    high = table.astype(np.float32).astype(ml_dtypes.bfloat16)
    low = (table - high.astype(np.float64)).astype(ml_dtypes.bfloat16)
    return high, low


def transform_tables(tokens):
    length = 2 * tokens
    rows = length // LANES
    half = rows // 2
    k1 = np.arange(half, dtype=np.float64) + 0.5
    n1 = np.arange(half, dtype=np.float64)
    n2 = np.arange(LANES, dtype=np.float64)
    outer = 2.0 * np.pi * k1[:, None] * n1[None, :] / rows
    cos, sin = np.cos(outer), np.sin(outer)
    first = np.concatenate([cos, -sin], axis=0)
    last = np.concatenate([cos.T, sin.T], axis=1) * (2.0 / length)
    twist = 2.0 * np.pi * k1[:, None] * n2[None, :] / length
    twists = np.concatenate([np.cos(twist), -np.sin(twist)], axis=1).astype(np.float32)
    inner = 2.0 * np.pi * n2[:, None] * n2[None, :] / LANES
    cos, sin = np.cos(inner), np.sin(inner)
    second = np.block([[cos, -sin], [sin, cos]])
    return split_table(first) + split_table(second) + split_table(last) + (twists,)


def gate_kernel(grad_out, query, key_proj, value, filter_param, out, go, q, k, v, filt, sems, *, filter_scale):
    f32 = jnp.float32
    channels, here = key_proj.shape
    pieces = here // LANES
    stride = 3 * pieces
    pairs = ((key_proj, k), (value, v), (grad_out, go), (query, q), (filter_param, filt))
    copies = [pltpu.make_async_copy(source, held, sems.at[i]) for i, (source, held) in enumerate(pairs)]
    for copy in copies:
        copy.start()

    def place(index, part):
        for piece in range(pieces):
            out[pl.ds(index * pieces + piece, channels, stride=stride), :] = part[:, piece * LANES : (piece + 1) * LANES]

    copies[0].wait()
    copies[1].wait()
    place(0, k[...].astype(f32) * v[...].astype(f32))
    copies[2].wait()
    copies[3].wait()
    place(1, go[...].astype(f32) * q[...].astype(f32))
    copies[4].wait()
    place(2, filt[...] * filter_scale)


def split(values):
    high = values.astype(jnp.bfloat16)
    low = (values - high.astype(jnp.float32)).astype(jnp.bfloat16)
    return high, low


def dot(left, right):
    return jnp.dot(left, right, preferred_element_type=jnp.float32)


def times_table(values, table):
    high, low = split(values)
    table_high, table_low = table
    return dot(high, table_high) + (dot(high, table_low) + dot(low, table_high))


def table_times(table, columns):
    table_high, table_low = table
    parts = [split(column) for column in columns]
    lows = dot(table_low, jnp.concatenate([high for high, _ in parts], axis=1))
    results = []
    for i, part in enumerate(parts):
        both = dot(table_high, jnp.concatenate(part, axis=1))
        results.append(both[:, :LANES] + (both[:, LANES:] + lows[:, i * LANES : (i + 1) * LANES]))
    return results


def turn(real, imag, twists):
    cos, sin = twists[:, :LANES], twists[:, LANES:]
    return jnp.concatenate([real * cos - imag * sin, real * sin + imag * cos], axis=1)


def forward(columns, first, second, twists):
    half = columns[0].shape[0]
    specs = [times_table(turn(mixed[:half], mixed[half:], twists), second) for mixed in table_times(first, columns)]
    return [(spec[:, :LANES], spec[:, LANES:]) for spec in specs]


def backward(spectra, second, last, twists):
    columns = []
    for spectrum in spectra:
        spec = times_table(jnp.concatenate(spectrum, axis=1), second)
        turned = turn(spec[:, :LANES], spec[:, LANES:], twists)
        columns.append(jnp.concatenate([turned[:, :LANES], turned[:, LANES:]], axis=0))
    return table_times(last, columns)


def spectral_kernel(
    taken, first_h, first_l, second_h, second_l, last_h, last_l, twists, timed, corr, held, sem, *, filter_scale
):
    shards, pieces, _ = corr.shape
    half = shards * pieces
    first, second, last = (first_h[...], first_l[...]), (second_h[...], second_l[...]), (last_h[...], last_l[...])
    columns = [taken[:, i * pieces : (i + 1) * pieces, :].reshape(half, LANES) for i in range(3)]
    (sig_re, sig_im), (cot_re, cot_im), (filt_re, filt_im) = forward(columns, first, second, twists[...])
    spectra = [
        (filt_re * sig_re - filt_im * sig_im, -(filt_re * sig_im + filt_im * sig_re)),
        (filt_re * cot_re + filt_im * cot_im, filt_im * cot_re - filt_re * cot_im),
    ]
    for i, part in enumerate(backward(spectra, second, last, twists[...])):
        held[:, i * pieces : (i + 1) * pieces, :] = part.reshape(shards, pieces, LANES)
    copy = pltpu.make_async_copy(held, timed, sem)
    copy.start()
    spectrum = (
        (cot_re * sig_re + cot_im * sig_im) * filter_scale,
        (cot_re * sig_im - cot_im * sig_re) * filter_scale,
    )
    (part,) = backward([spectrum], second, last, twists[...])
    corr[...] = part.reshape(shards, pieces, LANES)
    copy.wait()


def grads_kernel(
    back, grad_out, key_proj, value, total, swapped, grad_query, grad_key, grad_value, grad_filter
):
    f32 = jnp.float32
    channels, here = key_proj.shape
    pieces = here // LANES
    for piece in range(pieces):
        columns = slice(piece * LANES, (piece + 1) * LANES)
        rows = pl.ds(piece, channels, stride=pieces)
        grad_filter[:, columns] = total[rows, :] + swapped[rows, :]
        conv = back[pl.ds(piece, channels, stride=2 * pieces), :]
        grad_signal = back[pl.ds(pieces + piece, channels, stride=2 * pieces), :]
        grad_query[:, columns] = (grad_out[:, columns].astype(f32) * conv).astype(jnp.bfloat16)
        grad_key[:, columns] = (grad_signal * value[:, columns].astype(f32)).astype(jnp.bfloat16)
        grad_value[:, columns] = (grad_signal * key_proj[:, columns].astype(f32)).astype(jnp.bfloat16)


def local(grad_out, query, key_proj, value, filter_param):
    f32 = jnp.float32
    shards = lax.axis_size("ctx")
    groups = lax.axis_size("chan")
    channels, here = grad_out.shape
    tokens = shards * here
    pieces = here // LANES
    filter_scale = 1.0 / math.sqrt(tokens)
    params = pltpu.CompilerParams(vmem_limit_bytes=24 * 1024 * 1024)
    gated = pl.pallas_call(
        lambda *refs: gate_kernel(*refs, filter_scale=filter_scale),
        out_shape=jax.ShapeDtypeStruct((channels * 3 * pieces, LANES), f32),
        in_specs=[pl.BlockSpec(memory_space=pltpu.HBM)] * 5,
        scratch_shapes=[pltpu.VMEM((channels, here), jnp.bfloat16)] * 4
        + [pltpu.VMEM((channels, here), f32), pltpu.SemaphoreType.DMA((5,))],
        compiler_params=params,
        name="gate",
    )(*[pltpu.with_memory_space_constraint(each, pltpu.HBM) for each in (grad_out, query, key_proj, value, filter_param)])
    taken = lax.all_to_all(gated.reshape(channels, 3 * pieces, LANES), "ctx", 0, 0, tiled=True)
    tables = [jnp.asarray(table) for table in transform_tables(tokens)]
    timed, corr = pl.pallas_call(
        lambda *refs: spectral_kernel(*refs, filter_scale=filter_scale),
        out_shape=[
            jax.ShapeDtypeStruct((shards, 2 * pieces, LANES), f32),
            jax.ShapeDtypeStruct((shards, pieces, LANES), f32),
        ],
        out_specs=[pl.BlockSpec(memory_space=pltpu.HBM), pl.BlockSpec(memory_space=pltpu.VMEM)],
        scratch_shapes=[pltpu.VMEM((shards, 2 * pieces, LANES), f32), pltpu.SemaphoreType.DMA(())],
        compiler_params=params,
        name="spectral",
    )(taken, *tables)
    partial = lax.all_to_all(corr, "ctx", 0, 0, tiled=True).reshape(channels * pieces, LANES)
    back = lax.all_to_all(timed, "ctx", 0, 0, tiled=True)
    total = partial + lax.ppermute(partial, "chan", [(i, i ^ 2) for i in range(groups)])
    total = total + lax.ppermute(total, "chan", [(i, 2 * (groups // 2 - 1 - i // 2) + i % 2) for i in range(groups)])
    swapped = lax.ppermute(total, "chan", [(i, i ^ 1) for i in range(groups)])
    grad_query, grad_key, grad_value, grad_filter = pl.pallas_call(
        grads_kernel,
        out_shape=[jax.ShapeDtypeStruct((channels, here), jnp.bfloat16)] * 3
        + [jax.ShapeDtypeStruct((channels, here), f32)],
        compiler_params=params,
        name="grads",
    )(back.reshape(channels * 2 * pieces, LANES), grad_out, key_proj, value, total, swapped)
    return (grad_query, grad_key, grad_value, grad_filter)


def solution(mesh):
    split_spec = P("chan", "ctx")
    in_specs = (split_spec, split_spec, split_spec, split_spec, P(None, "ctx"))
    out_specs = (split_spec, split_spec, split_spec, P(None, "ctx"))
    return jax.shard_map(local, mesh=mesh, in_specs=in_specs, out_specs=out_specs, check_vma=False)
```

```python
import math

import jax
import jax.numpy as jnp
import ml_dtypes
import numpy as np
from jax import lax
from jax.experimental import pallas as pl
from jax.experimental.pallas import tpu as pltpu
from jax.sharding import PartitionSpec as P

LANES = 128
SUBLANES = 8


def split_table(table):
    high = table.astype(np.float32).astype(ml_dtypes.bfloat16)
    low = (table - high.astype(np.float64)).astype(ml_dtypes.bfloat16)
    return high, low


def transform_tables(tokens):
    length = 2 * tokens
    rows = length // LANES
    half = rows // 2
    k1 = np.arange(half, dtype=np.float64) + 0.5
    n1 = np.arange(half, dtype=np.float64)
    n2 = np.arange(LANES, dtype=np.float64)
    outer = 2.0 * np.pi * k1[:, None] * n1[None, :] / rows
    cos, sin = np.cos(outer), np.sin(outer)
    first = np.concatenate([cos, -sin], axis=0)
    last = np.concatenate([cos.T, sin.T], axis=1) * (2.0 / length)
    twist = 2.0 * np.pi * k1[:, None] * n2[None, :] / length
    twists = np.concatenate([np.cos(twist), -np.sin(twist)], axis=1).astype(np.float32)
    inner = 2.0 * np.pi * n2[:, None] * n2[None, :] / LANES
    cos, sin = np.cos(inner), np.sin(inner)
    second = np.block([[cos, -sin], [sin, cos]])
    return split_table(first) + split_table(second) + split_table(last) + (twists,)


def gate_kernel(grad_out, query, key_proj, value, filter_param, out, go, q, k, v, filt, sems, *, filter_scale):
    f32 = jnp.float32
    channels, here = key_proj.shape
    pieces = here // LANES
    stride = 3 * pieces
    pairs = ((key_proj, k), (value, v), (grad_out, go), (query, q), (filter_param, filt))
    copies = [pltpu.make_async_copy(source, held, sems.at[i]) for i, (source, held) in enumerate(pairs)]
    for copy in copies:
        copy.start()

    def place(index, part):
        for piece in range(pieces):
            out[pl.ds(index * pieces + piece, channels, stride=stride), :] = part[:, piece * LANES : (piece + 1) * LANES]

    copies[0].wait()
    copies[1].wait()
    place(0, k[...].astype(f32) * v[...].astype(f32))
    copies[2].wait()
    copies[3].wait()
    place(1, go[...].astype(f32) * q[...].astype(f32))
    copies[4].wait()
    place(2, filt[...] * filter_scale)


def split(values):
    high = values.astype(jnp.bfloat16)
    low = (values - high.astype(jnp.float32)).astype(jnp.bfloat16)
    return high, low


def dot(left, right):
    return jnp.dot(left, right, preferred_element_type=jnp.float32)


def times_table(values, table):
    high, low = split(values)
    table_high, table_low = table
    return dot(high, table_high) + (dot(high, table_low) + dot(low, table_high))


def table_times(table, columns):
    table_high, table_low = table
    parts = [split(column) for column in columns]
    lows = dot(table_low, jnp.concatenate([high for high, _ in parts], axis=1))
    results = []
    for i, part in enumerate(parts):
        both = dot(table_high, jnp.concatenate(part, axis=1))
        results.append(both[:, :LANES] + (both[:, LANES:] + lows[:, i * LANES : (i + 1) * LANES]))
    return results


def turn(real, imag, twists):
    cos, sin = twists[:, :LANES], twists[:, LANES:]
    return jnp.concatenate([real * cos - imag * sin, real * sin + imag * cos], axis=1)


def forward(columns, first, second, twists):
    half = columns[0].shape[0]
    specs = [times_table(turn(mixed[:half], mixed[half:], twists), second) for mixed in table_times(first, columns)]
    return [(spec[:, :LANES], spec[:, LANES:]) for spec in specs]


def backward(spectra, second, last, twists):
    columns = []
    for spectrum in spectra:
        spec = times_table(jnp.concatenate(spectrum, axis=1), second)
        turned = turn(spec[:, :LANES], spec[:, LANES:], twists)
        columns.append(jnp.concatenate([turned[:, :LANES], turned[:, LANES:]], axis=0))
    return table_times(last, columns)


def spectral_kernel(
    taken, first_h, first_l, second_h, second_l, last_h, last_l, twists, timed, corr, held, sem, *, filter_scale
):
    shards, pieces, _ = corr.shape
    half = shards * pieces
    first, second, last = (first_h[...], first_l[...]), (second_h[...], second_l[...]), (last_h[...], last_l[...])
    columns = [taken[:, i * pieces : (i + 1) * pieces, :].reshape(half, LANES) for i in range(3)]
    (sig_re, sig_im), (cot_re, cot_im), (filt_re, filt_im) = forward(columns, first, second, twists[...])
    spectra = [
        (filt_re * sig_re - filt_im * sig_im, -(filt_re * sig_im + filt_im * sig_re)),
        (filt_re * cot_re + filt_im * cot_im, filt_im * cot_re - filt_re * cot_im),
    ]
    for i, part in enumerate(backward(spectra, second, last, twists[...])):
        held[:, i * pieces : (i + 1) * pieces, :] = part.reshape(shards, pieces, LANES)
    copy = pltpu.make_async_copy(held, timed, sem)
    copy.start()
    spectrum = (
        (cot_re * sig_re + cot_im * sig_im) * filter_scale,
        (cot_re * sig_im - cot_im * sig_re) * filter_scale,
    )
    (part,) = backward([spectrum], second, last, twists[...])
    corr[...] = part.reshape(shards, pieces, LANES)
    copy.wait()


def grads_kernel(
    back, grad_out, key_proj, value, total, swapped, grad_query, grad_key, grad_value, grad_filter
):
    f32 = jnp.float32
    channels, here = key_proj.shape
    pieces = here // LANES
    for piece in range(pieces):
        columns = slice(piece * LANES, (piece + 1) * LANES)
        rows = pl.ds(piece, channels, stride=pieces)
        grad_filter[:, columns] = total[rows, :] + swapped[rows, :]
        conv = back[pl.ds(piece, channels, stride=2 * pieces), :]
        grad_signal = back[pl.ds(pieces + piece, channels, stride=2 * pieces), :]
        grad_query[:, columns] = (grad_out[:, columns].astype(f32) * conv).astype(jnp.bfloat16)
        grad_key[:, columns] = (grad_signal * value[:, columns].astype(f32)).astype(jnp.bfloat16)
        grad_value[:, columns] = (grad_signal * key_proj[:, columns].astype(f32)).astype(jnp.bfloat16)


def local(grad_out, query, key_proj, value, filter_param):
    f32 = jnp.float32
    shards = lax.axis_size("ctx")
    groups = lax.axis_size("chan")
    channels, here = grad_out.shape
    tokens = shards * here
    pieces = here // LANES
    filter_scale = 1.0 / math.sqrt(tokens)
    params = pltpu.CompilerParams(vmem_limit_bytes=24 * 1024 * 1024)
    gated = pl.pallas_call(
        lambda *refs: gate_kernel(*refs, filter_scale=filter_scale),
        out_shape=jax.ShapeDtypeStruct((channels * 3 * pieces, LANES), f32),
        in_specs=[pl.BlockSpec(memory_space=pltpu.HBM)] * 5,
        scratch_shapes=[pltpu.VMEM((channels, here), jnp.bfloat16)] * 4
        + [pltpu.VMEM((channels, here), f32), pltpu.SemaphoreType.DMA((5,))],
        compiler_params=params,
        name="gate",
    )(*[pltpu.with_memory_space_constraint(each, pltpu.HBM) for each in (grad_out, query, key_proj, value, filter_param)])
    taken = lax.all_to_all(gated.reshape(channels, 3 * pieces, LANES), "ctx", 0, 0, tiled=True)
    tables = [jnp.asarray(table) for table in transform_tables(tokens)]
    timed, corr = pl.pallas_call(
        lambda *refs: spectral_kernel(*refs, filter_scale=filter_scale),
        out_shape=[
            jax.ShapeDtypeStruct((shards, 2 * pieces, LANES), f32),
            jax.ShapeDtypeStruct((shards, pieces, LANES), f32),
        ],
        out_specs=[pl.BlockSpec(memory_space=pltpu.HBM), pl.BlockSpec(memory_space=pltpu.VMEM)],
        scratch_shapes=[pltpu.VMEM((shards, 2 * pieces, LANES), f32), pltpu.SemaphoreType.DMA(())],
        compiler_params=params,
        name="spectral",
    )(taken, *tables)
    partial = lax.all_to_all(corr, "ctx", 0, 0, tiled=True).reshape(channels * pieces, LANES)
    back = lax.all_to_all(timed, "ctx", 0, 0, tiled=True)
    def moved(values, bit):
        return lax.ppermute(values, "chan", [(i, i ^ bit) for i in range(groups)])

    total = partial + moved(partial, 1)
    total = total + moved(total, 2)
    swapped = moved(total, 4)
    grad_query, grad_key, grad_value, grad_filter = pl.pallas_call(
        grads_kernel,
        out_shape=[jax.ShapeDtypeStruct((channels, here), jnp.bfloat16)] * 3
        + [jax.ShapeDtypeStruct((channels, here), f32)],
        compiler_params=params,
        name="grads",
    )(back.reshape(channels * 2 * pieces, LANES), grad_out, key_proj, value, total, swapped)
    return (grad_query, grad_key, grad_value, grad_filter)


def solution(mesh):
    split_spec = P("chan", "ctx")
    in_specs = (split_spec, split_spec, split_spec, split_spec, P(None, "ctx"))
    out_specs = (split_spec, split_spec, split_spec, P(None, "ctx"))
    return jax.shard_map(local, mesh=mesh, in_specs=in_specs, out_specs=out_specs, check_vma=False)
```

```python
import math

import jax
import jax.numpy as jnp
import ml_dtypes
import numpy as np
from jax import lax
from jax.experimental import pallas as pl
from jax.experimental.pallas import tpu as pltpu
from jax.sharding import PartitionSpec as P

LANES = 128
SUBLANES = 8


def split_table(table):
    high = table.astype(np.float32).astype(ml_dtypes.bfloat16)
    low = (table - high.astype(np.float64)).astype(ml_dtypes.bfloat16)
    return high, low


def transform_tables(tokens):
    length = 2 * tokens
    rows = length // LANES
    half = rows // 2
    k1 = np.arange(half, dtype=np.float64) + 0.5
    n1 = np.arange(half, dtype=np.float64)
    n2 = np.arange(LANES, dtype=np.float64)
    outer = 2.0 * np.pi * k1[:, None] * n1[None, :] / rows
    cos, sin = np.cos(outer), np.sin(outer)
    first = np.concatenate([cos, -sin], axis=0)
    last = np.concatenate([cos.T, sin.T], axis=1) * (2.0 / length)
    twist = 2.0 * np.pi * k1[:, None] * n2[None, :] / length
    twists = np.concatenate([np.cos(twist), -np.sin(twist)], axis=1).astype(np.float32)
    inner = 2.0 * np.pi * n2[:, None] * n2[None, :] / LANES
    cos, sin = np.cos(inner), np.sin(inner)
    second = np.block([[cos, -sin], [sin, cos]])
    return split_table(first) + split_table(second) + split_table(last) + (twists,)


def gate_kernel(grad_out, query, key_proj, value, filter_param, out, go, q, k, v, filt, sems, *, filter_scale):
    f32 = jnp.float32
    channels, here = key_proj.shape
    pieces = here // LANES
    stride = 3 * pieces
    pairs = ((key_proj, k), (value, v), (grad_out, go), (query, q), (filter_param, filt))
    copies = [pltpu.make_async_copy(source, held, sems.at[i]) for i, (source, held) in enumerate(pairs)]
    for copy in copies:
        copy.start()

    def place(index, part):
        for piece in range(pieces):
            out[pl.ds(index * pieces + piece, channels, stride=stride), :] = part[:, piece * LANES : (piece + 1) * LANES]

    copies[0].wait()
    copies[1].wait()
    place(0, k[...].astype(f32) * v[...].astype(f32))
    copies[2].wait()
    copies[3].wait()
    place(1, go[...].astype(f32) * q[...].astype(f32))
    copies[4].wait()
    place(2, filt[...] * filter_scale)


def split(values):
    high = values.astype(jnp.bfloat16)
    low = (values - high.astype(jnp.float32)).astype(jnp.bfloat16)
    return high, low


def dot(left, right):
    return jnp.dot(left, right, preferred_element_type=jnp.float32)


def times_table(values, table):
    high, low = split(values)
    table_high, table_low = table
    return dot(high, table_high) + (dot(high, table_low) + dot(low, table_high))


def table_times(table, columns):
    table_high, table_low = table
    parts = [split(column) for column in columns]
    lows = dot(table_low, jnp.concatenate([high for high, _ in parts], axis=1))
    results = []
    for i, part in enumerate(parts):
        both = dot(table_high, jnp.concatenate(part, axis=1))
        results.append(both[:, :LANES] + (both[:, LANES:] + lows[:, i * LANES : (i + 1) * LANES]))
    return results


def turn(real, imag, twists):
    cos, sin = twists[:, :LANES], twists[:, LANES:]
    return jnp.concatenate([real * cos - imag * sin, real * sin + imag * cos], axis=1)


def forward(columns, first, second, twists):
    half = columns[0].shape[0]
    specs = [times_table(turn(mixed[:half], mixed[half:], twists), second) for mixed in table_times(first, columns)]
    return [(spec[:, :LANES], spec[:, LANES:]) for spec in specs]


def backward(spectra, second, last, twists):
    columns = []
    for spectrum in spectra:
        spec = times_table(jnp.concatenate(spectrum, axis=1), second)
        turned = turn(spec[:, :LANES], spec[:, LANES:], twists)
        columns.append(jnp.concatenate([turned[:, :LANES], turned[:, LANES:]], axis=0))
    return table_times(last, columns)


def spectral_kernel(
    taken, first_h, first_l, second_h, second_l, last_h, last_l, twists, timed, corr, held, sem, *, filter_scale
):
    shards, pieces, _ = corr.shape
    half = shards * pieces
    first, second, last = (first_h[...], first_l[...]), (second_h[...], second_l[...]), (last_h[...], last_l[...])
    columns = [taken[:, i * pieces : (i + 1) * pieces, :].reshape(half, LANES) for i in range(3)]
    (sig_re, sig_im), (cot_re, cot_im), (filt_re, filt_im) = forward(columns, first, second, twists[...])
    spectra = [
        (filt_re * sig_re - filt_im * sig_im, -(filt_re * sig_im + filt_im * sig_re)),
        (filt_re * cot_re + filt_im * cot_im, filt_im * cot_re - filt_re * cot_im),
    ]
    for i, part in enumerate(backward(spectra, second, last, twists[...])):
        held[:, i * pieces : (i + 1) * pieces, :] = part.reshape(shards, pieces, LANES)
    copy = pltpu.make_async_copy(held, timed, sem)
    copy.start()
    spectrum = (
        (cot_re * sig_re + cot_im * sig_im) * filter_scale,
        (cot_re * sig_im - cot_im * sig_re) * filter_scale,
    )
    (part,) = backward([spectrum], second, last, twists[...])
    corr[...] = part.reshape(shards, pieces, LANES)
    copy.wait()


def grads_kernel(
    back, grad_out, key_proj, value, total, swapped, grad_query, grad_key, grad_value, grad_filter, gq, gk, gv, gf, sems
):
    f32 = jnp.float32
    channels, here = key_proj.shape
    pieces = here // LANES
    blocks = [slice(piece * LANES, (piece + 1) * LANES) for piece in range(pieces)]
    copies = []

    def send(held, target):
        copies.append(pltpu.make_async_copy(held, target, sems.at[len(copies)]))
        copies[-1].start()

    for piece, columns in enumerate(blocks):
        rows = pl.ds(piece, channels, stride=pieces)
        gf[:, columns] = total[rows, :] + swapped[rows, :]
    send(gf, grad_filter)
    for piece, columns in enumerate(blocks):
        conv = back[pl.ds(piece, channels, stride=2 * pieces), :]
        gq[:, columns] = (grad_out[:, columns].astype(f32) * conv).astype(jnp.bfloat16)
    send(gq, grad_query)
    for piece, columns in enumerate(blocks):
        grad_signal = back[pl.ds(pieces + piece, channels, stride=2 * pieces), :]
        gk[:, columns] = (grad_signal * value[:, columns].astype(f32)).astype(jnp.bfloat16)
        gv[:, columns] = (grad_signal * key_proj[:, columns].astype(f32)).astype(jnp.bfloat16)
    send(gk, grad_key)
    send(gv, grad_value)
    for copy in copies:
        copy.wait()


def local(grad_out, query, key_proj, value, filter_param):
    f32 = jnp.float32
    shards = lax.axis_size("ctx")
    groups = lax.axis_size("chan")
    channels, here = grad_out.shape
    tokens = shards * here
    pieces = here // LANES
    filter_scale = 1.0 / math.sqrt(tokens)
    params = pltpu.CompilerParams(vmem_limit_bytes=24 * 1024 * 1024)
    gated = pl.pallas_call(
        lambda *refs: gate_kernel(*refs, filter_scale=filter_scale),
        out_shape=jax.ShapeDtypeStruct((channels * 3 * pieces, LANES), f32),
        in_specs=[pl.BlockSpec(memory_space=pltpu.HBM)] * 5,
        scratch_shapes=[pltpu.VMEM((channels, here), jnp.bfloat16)] * 4
        + [pltpu.VMEM((channels, here), f32), pltpu.SemaphoreType.DMA((5,))],
        compiler_params=params,
        name="gate",
    )(*[pltpu.with_memory_space_constraint(each, pltpu.HBM) for each in (grad_out, query, key_proj, value, filter_param)])
    taken = lax.all_to_all(gated.reshape(channels, 3 * pieces, LANES), "ctx", 0, 0, tiled=True)
    tables = [jnp.asarray(table) for table in transform_tables(tokens)]
    timed, corr = pl.pallas_call(
        lambda *refs: spectral_kernel(*refs, filter_scale=filter_scale),
        out_shape=[
            jax.ShapeDtypeStruct((shards, 2 * pieces, LANES), f32),
            jax.ShapeDtypeStruct((shards, pieces, LANES), f32),
        ],
        out_specs=[pl.BlockSpec(memory_space=pltpu.HBM), pl.BlockSpec(memory_space=pltpu.VMEM)],
        scratch_shapes=[pltpu.VMEM((shards, 2 * pieces, LANES), f32), pltpu.SemaphoreType.DMA(())],
        compiler_params=params,
        name="spectral",
    )(taken, *tables)
    partial = lax.all_to_all(corr, "ctx", 0, 0, tiled=True).reshape(channels * pieces, LANES)
    back = lax.all_to_all(timed, "ctx", 0, 0, tiled=True)
    def moved(values, bit):
        return lax.ppermute(values, "chan", [(i, i ^ bit) for i in range(groups)])

    total = partial + moved(partial, 1)
    total = total + moved(total, 2)
    swapped = moved(total, 4)
    grad_query, grad_key, grad_value, grad_filter = pl.pallas_call(
        grads_kernel,
        out_shape=[jax.ShapeDtypeStruct((channels, here), jnp.bfloat16)] * 3
        + [jax.ShapeDtypeStruct((channels, here), f32)],
        out_specs=[pl.BlockSpec(memory_space=pltpu.HBM)] * 4,
        scratch_shapes=[pltpu.VMEM((channels, here), jnp.bfloat16)] * 3
        + [pltpu.VMEM((channels, here), f32), pltpu.SemaphoreType.DMA((4,))],
        compiler_params=params,
        name="grads",
    )(back.reshape(channels * 2 * pieces, LANES), grad_out, key_proj, value, total, swapped)
    return (grad_query, grad_key, grad_value, grad_filter)


def solution(mesh):
    split_spec = P("chan", "ctx")
    in_specs = (split_spec, split_spec, split_spec, split_spec, P(None, "ctx"))
    out_specs = (split_spec, split_spec, split_spec, P(None, "ctx"))
    return jax.shard_map(local, mesh=mesh, in_specs=in_specs, out_specs=out_specs, check_vma=False)
```
